256 devices in a mesh: dp: 64 (over x, z, core), seq: 4 (over y).
Axes of the slice: x: 4, y: 4, z: 8, core: 2. Of those that a mesh axis runs over, the one named last changes fastest.
Arguments:
- tokens: bfloat16 [256, 6144], P('dp', 'seq'), may hold values from -6 to 6
- expert_ids: int32 [256, 2], P('dp'), may hold values from 0 to 7, all different within a row; in each aligned block of 4 rows (0 to 3, 4 to 7, ...) at most 2 rows name the same one
- router: bfloat16 [6144, 8], P('seq'), may hold values from -0.21875 to 0.21875
- w_gate: bfloat16 [5, 6144, 16384], P(None, 'seq', 'dp'), may hold values from -0.078125 to 0.078125
- w_up: bfloat16 [5, 6144, 16384], P(None, 'seq', 'dp'), may hold values from -0.078125 to 0.078125
- w_down: bfloat16 [5, 16384, 6144], P(None, 'dp', 'seq'), may hold values from -0.046875 to 0.046875
Outputs:
- mixed: bfloat16 [256, 6144], P('dp', 'seq')
The draws below stay inside these ranges and needn't reach their ends.
Inputs may be any that keep to these rules, and one draw needn't show every extreme that they name: `expert_ids`: each row names 2 different experts. The 4 tokens of one index of dp name any expert at most 2 times, a bound that some block reaches.
All inputs are finite; a program needn't handle non-finite values.
Results may differ from the reference program's by a relative error of at most 0.0049.
Values may be sent and summed in bfloat16 or wider, within the bound.
A program may use at most 64 MiB of HBM per device.

```python
import math
import jax
import jax.numpy as jnp
import numpy as np

D = 6144
FF = 16384
EXPERTS = 8
TOP = 2
WINDOW = 5
TOK_DEV = 4
MOST = 2
TOKENS = 256
N_DP = 64


def block_levels(rng, shape, pieces, smallest, largest):
    factor_of, own = 1.0, jax.random.fold_in(rng, 6)
    for dim, parts in pieces:
        steps = jnp.exp(jax.random.uniform(jax.random.fold_in(own, dim), (parts,), jnp.float32, smallest / len(pieces), largest / len(pieces)))
        factor_of = factor_of * jnp.repeat(steps, shape[dim] // parts).reshape([-1 if axis == dim else 1 for axis in range(len(shape))])
    return factor_of


def deal_out(own_key, own, number, rows, amount, top, most, skew):
    order = jax.random.permutation(own_key, amount)
    crowded, ordinary = shares(amount, rows * top, most, skew, True), shares(amount, rows * top, most, skew, False)
    places = jnp.arange(amount)

    def named(sizes, rotation):
        used = int((sizes > 0).sum())
        fixed = max(1, used // 4)
        passed = fixed + (places - fixed + rotation * (used - fixed)) % max(1, amount - fixed)
        return jnp.zeros((amount,), jnp.int32).at[order[jnp.where(places < fixed, places, passed)]].set(jnp.asarray(sizes, jnp.int32))

    sizes = jnp.where(number % 4 == 0, named(crowded, number // 4), named(ordinary, number - number // 4 - 1))
    mixed = jax.random.permutation(jax.random.fold_in(own, 3), amount)
    giver, sink = mixed[0:amount // 2 * 2:2], mixed[1:amount // 2 * 2:2]
    room = jnp.minimum(sizes[giver] - 1, most - sizes[sink]) // 2
    room = jnp.where((giver == order[0]) | (sink == order[0]) | (sizes[sink] == 0), 0, jnp.maximum(room, 0))
    passed = jax.random.randint(jax.random.fold_in(own, 4), (amount // 2,), 0, 1 << 20) % (room + 1)
    sizes = sizes.at[giver].add(-passed).at[sink].add(passed)
    labels = jnp.searchsorted(jnp.cumsum(sizes), jnp.arange(rows * top), side="right").astype(jnp.int32)
    listing = labels.reshape(top, rows).T
    listing = listing[jax.random.permutation(jax.random.fold_in(own, 1), rows)]
    rotation = jax.random.randint(jax.random.fold_in(own, 2), (rows, 1), 0, top)
    return jnp.take_along_axis(listing, (jnp.arange(top)[None, :] + rotation) % top, axis=1)


def shares(amount, total, reach, lean, full):
    weights = [(1 << 20) // math.isqrt(rank ** lean) + 1 for rank in range(1, amount + 1)]
    largest = reach if full else min(reach, max(-(-total // amount), total * weights[0] // sum(weights)))
    least = 1 if total - largest >= amount - 1 else 0
    given, surplus = [largest] + [least] * (amount - 1), total - largest - least * (amount - 1)
    while surplus > 0:
        candidates = [i for i in range(1, amount) if given[i] < largest] or [i for i in range(1, amount) if given[i] < reach]
        whole, left = sum([weights[i] for i in candidates]), surplus
        for i in candidates:
            extra = min(reach - given[i], max(1, left * weights[i] // whole), surplus)
            given[i] = given[i] + extra
            surplus = surplus - extra
    return np.array(given)


def scatter_about(rng, dims, deviation, bound, shards=(), held_as=jnp.bfloat16):
    factor_of = block_levels(rng, dims, shards, -0.22, 0.18) if shards else 1.0
    drawn = jax.random.normal(rng, dims, jnp.float32) * deviation * factor_of
    return jnp.minimum(jnp.maximum(drawn, -bound), bound).astype(held_as)


def setup_inputs(seed: int = 0) -> dict:
    key_list = jax.random.split(jax.random.key(seed), 7)
    tokens = scatter_about(key_list[0], (TOKENS, D), 1.0, 6.0, ((0, 64), (1, 4)))
    expert_ids_keys = jax.random.split(jax.random.fold_in(key_list[1], 1), TOKENS // TOK_DEV)
    expert_ids_turns = jax.random.permutation(jax.random.fold_in(key_list[1], 3), TOKENS // TOK_DEV)
    expert_ids = jax.vmap(lambda own, number: deal_out(jax.random.fold_in(key_list[1], 2), own, number, TOK_DEV, EXPERTS, TOP, MOST, 2))(expert_ids_keys, expert_ids_turns).reshape((TOKENS, TOP))
    router = scatter_about(key_list[2], (D, EXPERTS), (D // 9) ** -0.5, 0.21875, ((0, 4),))
    w_gate = scatter_about(key_list[3], (WINDOW, D, FF), D ** -0.5, 0.078125, ((1, 4), (2, 64)))
    w_up = scatter_about(key_list[4], (WINDOW, D, FF), D ** -0.5, 0.078125, ((1, 4), (2, 64)))
    w_down = scatter_about(key_list[5], (WINDOW, FF, D), FF ** -0.5, 0.046875, ((1, 64), (2, 4)))
    return {"tokens": tokens, "expert_ids": expert_ids, "router": router, "w_gate": w_gate, "w_up": w_up, "w_down": w_down}


def expert_rows(expert_ids, expert, capacity):
    member = jnp.any(expert_ids == expert, axis=1)
    position = jnp.cumsum(member.astype(jnp.int32)) - 1
    target = jnp.where(member, position, capacity).astype(jnp.int32)
    count_all = expert_ids.shape[0]
    row_token = jnp.zeros((capacity,), jnp.int32).at[target].set(jnp.arange(count_all, dtype=jnp.int32), mode="drop")
    return row_token, jnp.maximum(position, 0).astype(jnp.int32)


def reference(tokens, expert_ids, router, w_gate, w_up, w_down):
    capacity = MOST * N_DP
    logits = jnp.dot(tokens, router, preferred_element_type=jnp.float32)
    chosen = jnp.take_along_axis(logits, expert_ids, axis=1)
    share_first = 1.0 / (1.0 + jnp.exp(chosen[:, 1] - chosen[:, 0]))
    share_second = 1.0 / (1.0 + jnp.exp(chosen[:, 0] - chosen[:, 1]))
    totals = jnp.zeros(tokens.shape, jnp.float32)
    for expert in range(WINDOW):
        row_token, position = expert_rows(expert_ids, expert, capacity)
        buffer = tokens[row_token]
        gate_part = jnp.dot(buffer, w_gate[expert], preferred_element_type=jnp.float32)
        up_part = jnp.dot(buffer, w_up[expert], preferred_element_type=jnp.float32)
        hidden = (jax.nn.silu(gate_part) * up_part).astype(jnp.bfloat16)
        expert_out = jnp.dot(hidden, w_down[expert], preferred_element_type=jnp.float32)
        weighting = jnp.where(expert_ids[:, 0] == expert, share_first, jnp.float32(0.0))
        weighting = weighting + jnp.where(expert_ids[:, 1] == expert, share_second, jnp.float32(0.0))
        totals = totals + weighting[:, None] * expert_out[position]
    return totals.astype(jnp.bfloat16)
```

```python
import functools

import jax
import jax.numpy as jnp
from jax import lax
from jax.experimental import pallas as pl
from jax.experimental.pallas import tpu as pltpu
from jax.sharding import PartitionSpec as P

NX, NZ, NC, NY = 4, 8, 2, 4
EXPERTS = 8
WINDOW = 5
TOK = 4
TOKENS = TOK * NX * NZ * NC
DS = 1536
HID = 256
HALF = DS // 2
COLS = 256
PARTS = HALF // COLS
MSG = DS + 128
ROWS_Y = TOKENS // NY
ROWS_X = TOKENS // NX
ROWS_Z = ROWS_X // NZ
Z_ORDER = (1, 7, 2, 6, 3, 5, 4)
F32, BF16 = jnp.float32, jnp.bfloat16


def kernel(
    tokens_ref, ids_ref, router_ref, wg_ref, wu_ref, wd_ref, out_ref,
    xb, x2d, wg, wu, wd, lg_own, lg_got, yacc, ysend, ygot, hid, abuf,
    f1send, f1got, own, f2send, f2got, f3own, f3send, f3got, f4send, f4got,
    tok_sem, w_sem, zs, zr, xs, xr, cs, cr, ls, lr, ys, yr, hs, hr,
    f1s, f1r, f2s, f2r, f3s, f3r, f4s, f4r,
):
    d, s = lax.axis_index("dp"), lax.axis_index("seq")
    c = lax.rem(d, NC)
    z = lax.rem(lax.div(d, NC), NZ)
    x = lax.div(d, NC * NZ)

    def dev(px, pz, pc, ps):
        return ((px * NZ + pz) * NC + pc, ps)

    def around(v, o, n):
        return lax.rem(v + (o + n), n)

    sibling = dev(x, z, 1 - c, s)
    z_peer = {o: dev(x, around(z, o, NZ), c, s) for o in range(1, NZ)}
    x_peer = {o: dev(around(x, o, NX), z, c, s) for o in range(1, NX)}
    y_peer = {o: dev(x, z, c, around(s, o, NY)) for o in range(1, NY)}
    sent = []

    def send(src, dst, ssem, rsem, to):
        cp = pltpu.make_async_remote_copy(
            src_ref=src, dst_ref=dst, send_sem=ssem, recv_sem=rsem,
            device_id=to, device_id_type=pl.DeviceIdType.MESH)
        cp.start()
        sent.append(cp)

    def arrived(dst, ssem, rsem):
        pltpu.make_async_remote_copy(
            src_ref=dst, dst_ref=dst, send_sem=ssem, recv_sem=rsem,
            device_id=sibling, device_id_type=pl.DeviceIdType.MESH).wait_recv()

    mine = xb.at[x, z, c]
    tok_copy = pltpu.make_async_copy(tokens_ref, mine.at[:, pl.ds(0, DS)], tok_sem)
    tok_copy.start()

    barrier = pltpu.get_barrier_semaphore()
    peers = [sibling, *z_peer.values(), *x_peer.values(), *y_peer.values()]
    for peer in peers:
        pl.semaphore_signal(barrier, inc=1, device_id=peer, device_id_type=pl.DeviceIdType.MESH)

    w_copies = []
    for e in range(WINDOW):
        for i, (src, dst) in enumerate(((wg_ref, wg), (wu_ref, wu))):
            w_copies.append(pltpu.make_async_copy(src.at[e], dst.at[e], w_sem.at[i, e]))
    for e in range(WINDOW):
        w_copies.append(pltpu.make_async_copy(wd_ref.at[e], wd.at[e], w_sem.at[2, e]))
    for cp in w_copies:
        cp.start()

    row = lax.broadcasted_iota(jnp.int32, (TOK, 128), 0)
    lane = lax.broadcasted_iota(jnp.int32, (TOK, 128), 1)
    named = jnp.zeros((TOK, 128), jnp.int32)
    for t in range(TOK):
        for k in range(2):
            named = jnp.where((row == t) & (lane == k), ids_ref[k, t], named)
    xb[x, z, c, :, DS:MSG] = named.astype(F32).astype(BF16)

    tok_copy.wait()
    pl.semaphore_wait(barrier, len(peers))

    with jax.named_scope("gather"):
        for o in Z_ORDER:
            send(mine, mine, zs.at[o - 1], zr.at[o - 1], z_peer[o])
        for p in range(1, NX):
            send(mine, mine, xs.at[p - 1, 0], xr.at[p - 1], x_peer[p])
        for o in Z_ORDER:
            block = xb.at[x, around(z, -o, NZ), c]
            arrived(block, zs.at[o - 1], zr.at[o - 1])
            for p in range(1, NX):
                send(block, block, xs.at[p - 1, o], xr.at[p - 1], x_peer[p])
        line = xb.at[x, :, c]
        send(line, line, cs.at[0], cr.at[0], sibling)
        for p in (1, 3, 2):
            line = xb.at[around(x, -p, NX), :, c]
            arrived(line, cs.at[0], xr.at[p - 1])
            send(line, line, cs.at[p], cr.at[p], sibling)
        for p in (0, 1, 3, 2):
            line = xb.at[around(x, -p, NX), :, 1 - c]
            arrived(line, cs.at[0], cr.at[p])

    x2d[...] = xb[:, :, :, :, 0:DS].reshape(TOKENS, DS)
    ids = xb[:, :, :, :, DS:MSG].reshape(TOKENS, 128).astype(F32)
    first, second = ids[:, 0:1], ids[:, 1:2]

    with jax.named_scope("logits"):
        lg_own[...] = lax.dot_general(
            router_ref[...], x2d[...], (((1,), (1,)), ((), ())), preferred_element_type=F32)
        for p in range(1, NY):
            send(lg_own, lg_got.at[p - 1], ls.at[p - 1], lr.at[p - 1], y_peer[p])

    with jax.named_scope("gate_up"):
        for e in range(WINDOW):
            for i, w in enumerate((wg, wu)):
                w_copies[2 * e + i].wait()
                product = jnp.dot(x2d[...], w[e], preferred_element_type=F32)
                for k, named in enumerate((first, second)):
                    before = yacc[k, :, i * HID:(i + 1) * HID] if e else jnp.zeros((TOKENS, HID), F32)
                    yacc[k, :, i * HID:(i + 1) * HID] = jnp.where(named == float(e), product, before)
        for q in range(NY):
            for k in range(2):
                ysend[q, k] = yacc[k, q * ROWS_Y:(q + 1) * ROWS_Y, :].astype(BF16)
        for p in (2, 1, 3):
            send(ysend.at[around(s, p, NY)], ygot.at[p - 1], ys.at[p - 1], yr.at[p - 1], y_peer[p])

    with jax.named_scope("shares"):
        logits = lg_own[...]
        for p in range(1, NY):
            arrived(lg_got.at[p - 1], ls.at[0], lr.at[p - 1])
            logits = logits + lg_got[p - 1]
        logits = logits.T
        expert = lax.broadcasted_iota(jnp.int32, (TOKENS, EXPERTS), 1).astype(F32)
        a = jnp.sum(jnp.where(expert == first, logits, 0.0), axis=1, keepdims=True)
        b = jnp.sum(jnp.where(expert == second, logits, 0.0), axis=1, keepdims=True)
        share_first = 1.0 / (1.0 + jnp.exp(b - a))
        share_second = 1.0 / (1.0 + jnp.exp(a - b))

    with jax.named_scope("hidden"):
        for p in (1, 3, 2):
            arrived(ygot.at[p - 1], ys.at[0], yr.at[p - 1])
        for k in range(2):
            total = yacc[k, pl.ds(pl.multiple_of(s * ROWS_Y, ROWS_Y), ROWS_Y), :]
            for p in range(1, NY):
                total = total + ygot[p - 1, k].astype(F32)
            gate, up = total[:, :HID], total[:, HID:]
            hid[s, k] = (gate / (1.0 + jnp.exp(-gate)) * up).astype(BF16)
        for p in (2, 1, 3):
            send(hid.at[s], hid.at[s], hs.at[p - 1], hr.at[p - 1], y_peer[p])
        for p in (1, 3, 2):
            arrived(hid.at[around(s, -p, NY)], hs.at[0], hr.at[p - 1])
        h0 = hid[:, 0].reshape(TOKENS, HID).astype(F32)
        h1 = hid[:, 1].reshape(TOKENS, HID).astype(F32)
        for e in range(WINDOW):
            abuf[e] = jnp.where(first == float(e), h0, jnp.where(second == float(e), h1, 0.0)).astype(BF16)

    with jax.named_scope("down"):
        for e in range(WINDOW):
            w_copies[2 * WINDOW + e].wait()
        for mine_now in (False, True):
            base = (c if mine_now else 1 - c) * HALF
            for n in range(PARTS):
                columns = pl.ds(pl.multiple_of(base + n * COLS, COLS), COLS)
                total = None
                for e in range(WINDOW):
                    weight = jnp.where(first == float(e), share_first, 0.0)
                    weight = weight + jnp.where(second == float(e), share_second, 0.0)
                    term = weight * jnp.dot(abuf[e], wd[e, :, columns], preferred_element_type=F32)
                    total = term if total is None else total + term
                if not mine_now:
                    f1send[n] = total
                    send(f1send.at[n], f1got.at[n], f1s.at[n], f1r.at[n], sibling)
                else:
                    arrived(f1got.at[n], f1s.at[n], f1r.at[n])
                    total = total + f1got[n]
                    own[n] = total
                    for q in range(NX):
                        f2send[n, q] = total[q * ROWS_X:(q + 1) * ROWS_X, :].astype(BF16)
                    for p in (2, 1, 3):
                        send(f2send.at[n, around(x, p, NX)], f2got.at[n, p - 1],
                             f2s.at[n, p - 1], f2r.at[n, p - 1], x_peer[p])

    with jax.named_scope("along_x"):
        for n in range(PARTS):
            total = own[n, pl.ds(pl.multiple_of(x * ROWS_X, ROWS_X), ROWS_X), :]
            for p in (1, 3, 2):
                arrived(f2got.at[n, p - 1], f2s.at[n, p - 1], f2r.at[n, p - 1])
                total = total + f2got[n, p - 1].astype(F32)
            total = total.reshape(NZ, ROWS_Z, COLS)
            f3own[:, :, n * COLS:(n + 1) * COLS] = total
            f3send[:, :, n * COLS:(n + 1) * COLS] = total.astype(BF16)

    with jax.named_scope("along_z"):
        for o in (4, 3, 5, 2, 6, 1, 7):
            send(f3send.at[around(z, o, NZ)], f3got.at[o - 1], f3s.at[o - 1], f3r.at[o - 1], z_peer[o])
        total = f3own[z]
        for o in Z_ORDER:
            arrived(f3got.at[o - 1], f3s.at[o - 1], f3r.at[o - 1])
            total = total + f3got[o - 1].astype(F32)
        upper, lower = total[:TOK].astype(BF16), total[TOK:].astype(BF16)
        f4send[...] = jnp.where(c == 0, lower, upper)
        send(f4send, f4got, f4s, f4r, sibling)
        kept = jnp.where(c == 0, upper, lower)
        arrived(f4got, f4s, f4r)
        other = f4got[...]
        out_ref[:, 0:HALF] = jnp.where(c == 0, kept, other)
        out_ref[:, HALF:DS] = jnp.where(c == 0, other, kept)

    for cp in sent:
        cp.wait_send()


def body(tokens, expert_ids, router, w_gate, w_up, w_down):
    vmem, hbm = pl.BlockSpec(memory_space=pltpu.VMEM), pl.BlockSpec(memory_space=pl.ANY)
    dma = pltpu.SemaphoreType.DMA
    scratch = [
        pltpu.VMEM((NX, NZ, NC, TOK, MSG), BF16),
        pltpu.VMEM((TOKENS, DS), BF16),
        pltpu.VMEM((WINDOW, DS, HID), BF16),
        pltpu.VMEM((WINDOW, DS, HID), BF16),
        pltpu.VMEM((WINDOW, HID, DS), BF16),
        pltpu.VMEM((EXPERTS, TOKENS), F32),
        pltpu.VMEM((NY - 1, EXPERTS, TOKENS), F32),
        pltpu.VMEM((2, TOKENS, 2 * HID), F32),
        pltpu.VMEM((NY, 2, ROWS_Y, 2 * HID), BF16),
        pltpu.VMEM((NY - 1, 2, ROWS_Y, 2 * HID), BF16),
        pltpu.VMEM((NY, 2, ROWS_Y, HID), BF16),
        pltpu.VMEM((WINDOW, TOKENS, HID), BF16),
        pltpu.VMEM((PARTS, TOKENS, COLS), F32),
        pltpu.VMEM((PARTS, TOKENS, COLS), F32),
        pltpu.VMEM((PARTS, TOKENS, COLS), F32),
        pltpu.VMEM((PARTS, NX, ROWS_X, COLS), BF16),
        pltpu.VMEM((PARTS, NX - 1, ROWS_X, COLS), BF16),
        pltpu.VMEM((NZ, ROWS_Z, HALF), F32),
        pltpu.VMEM((NZ, ROWS_Z, HALF), BF16),
        pltpu.VMEM((NZ - 1, ROWS_Z, HALF), BF16),
        pltpu.VMEM((TOK, HALF), BF16),
        pltpu.VMEM((TOK, HALF), BF16),
        dma, dma((3, WINDOW)),
        dma((NZ - 1,)), dma((NZ - 1,)),
        dma((NX - 1, NZ)), dma((NX - 1,)),
        dma((NX,)), dma((NX,)),
        dma((NY - 1,)), dma((NY - 1,)),
        dma((NY - 1,)), dma((NY - 1,)),
        dma((NY - 1,)), dma((NY - 1,)),
        dma((PARTS,)), dma((PARTS,)),
        dma((PARTS, NX - 1)), dma((PARTS, NX - 1)),
        dma((NZ - 1,)), dma((NZ - 1,)),
        dma, dma,
    ]
    flops = 6 * WINDOW * TOKENS * DS * HID
    return pl.pallas_call(
        kernel,
        out_shape=jax.ShapeDtypeStruct((TOK, DS), BF16),
        in_specs=[hbm, pl.BlockSpec(memory_space=pltpu.SMEM), vmem, hbm, hbm, hbm],
        out_specs=vmem,
        scratch_shapes=scratch,
        compiler_params=pltpu.CompilerParams(
            collective_id=0, has_side_effects=True, vmem_limit_bytes=60 * 1024 * 1024),
        cost_estimate=pl.CostEstimate(flops=flops, bytes_accessed=6 * WINDOW * DS * HID, transcendentals=0),
    )(tokens, expert_ids.T, router.T, w_gate, w_up, w_down)


def solution(mesh):
    placed = (
        P("dp", "seq"),
        P("dp", None),
        P("seq", None),
        P(None, "seq", "dp"),
        P(None, "seq", "dp"),
        P(None, "dp", "seq"),
    )
    return jax.shard_map(
        body, mesh=mesh, in_specs=placed, out_specs=P("dp", "seq"), check_vma=False
    )
```

```python
import functools

import jax
import jax.numpy as jnp
from jax import lax
from jax.experimental import pallas as pl
from jax.experimental.pallas import tpu as pltpu
from jax.sharding import PartitionSpec as P

NX, NZ, NC, NY = 4, 8, 2, 4
EXPERTS = 8
WINDOW = 5
TOK = 4
TOKENS = TOK * NX * NZ * NC
CORE_ROWS = TOKENS // NC
DS = 1536
HID = 256
CHUNKS = 2
HCOL = HID // CHUNKS
PARTS = 3
COLS = DS // PARTS
TILE = 256
MSG = DS + 128
ROWS_Y = TOKENS // NY
ROWS_X = CORE_ROWS // NX
Z_ORDER = (1, 7, 2, 6, 3, 5, 4)
ALL_Z = (0, *Z_ORDER)
F32, BF16 = jnp.float32, jnp.bfloat16


def kernel(
    tokens_ref, ids_hbm, router_hbm, wg_ref, wu_ref, wd_ref, out_ref,
    xb, x2d, wg, wu, wd, router_ref, ids_ref, lg_own, lg_got, yacc, ysend, ygot, hid, abuf,
    pbuf, f1got, f2send, f2got, f3own, f3send, f3got,
    tok_sem, id_sem, router_sem, w_sem, zs, zr, xs, xr, cs, cr, ls, lr, ys, yr, hs, hr,
    f1s, f1r, f2s, f2r, f3s, f3r,
):
    d, s = lax.axis_index("dp"), lax.axis_index("seq")
    c = lax.rem(d, NC)
    z = lax.rem(lax.div(d, NC), NZ)
    x = lax.div(d, NC * NZ)

    def dev(px, pz, pc, ps):
        return ((px * NZ + pz) * NC + pc, ps)

    def around(v, o, n):
        return lax.rem(v + (o + n), n)

    sibling = dev(x, z, 1 - c, s)
    z_peer = {o: dev(x, around(z, o, NZ), c, s) for o in range(1, NZ)}
    x_peer = {o: dev(around(x, o, NX), z, c, s) for o in range(1, NX)}
    y_peer = {o: dev(x, z, c, around(s, o, NY)) for o in range(1, NY)}
    peers = [sibling, *z_peer.values(), *x_peer.values(), *y_peer.values()]
    sent = []

    def send(src, dst, ssem, rsem, to):
        cp = pltpu.make_async_remote_copy(
            src_ref=src, dst_ref=dst, send_sem=ssem, recv_sem=rsem,
            device_id=to, device_id_type=pl.DeviceIdType.MESH)
        cp.start()
        sent.append(cp)

    def arrived(dst, rsem):
        pltpu.make_async_remote_copy(
            src_ref=dst, dst_ref=dst, send_sem=rsem, recv_sem=rsem,
            device_id=sibling, device_id_type=pl.DeviceIdType.MESH).wait_recv()

    barrier = pltpu.get_barrier_semaphore()
    for peer in peers:
        pl.semaphore_signal(barrier, inc=1, device_id=peer, device_id_type=pl.DeviceIdType.MESH)

    mine = xb.at[c, x, z]
    id_copy = pltpu.make_async_copy(ids_hbm, ids_ref, id_sem)
    tok_copy = pltpu.make_async_copy(tokens_ref, mine.at[:, pl.ds(0, DS)], tok_sem)
    router_copy = pltpu.make_async_copy(router_hbm, router_ref, router_sem)
    w_copies = []
    for e in range(WINDOW):
        for i, (src, dst) in enumerate(((wg_ref, wg), (wu_ref, wu))):
            w_copies.append(pltpu.make_async_copy(src.at[e], dst.at[e], w_sem.at[i, e]))
    for e in range(WINDOW):
        w_copies.append(pltpu.make_async_copy(wd_ref.at[e], wd.at[e], w_sem.at[2, e]))
    for cp in (id_copy, tok_copy, router_copy, *w_copies):
        cp.start()

    id_copy.wait()
    row = lax.broadcasted_iota(jnp.int32, (TOK, 128), 0)
    lane = lax.broadcasted_iota(jnp.int32, (TOK, 128), 1)
    named = jnp.zeros((TOK, 128), jnp.int32)
    for t in range(TOK):
        for k in range(2):
            named = jnp.where((row == t) & (lane == k), ids_ref[k, t], named)
    xb[c, x, z, :, DS:MSG] = named.astype(F32).astype(BF16)
    tok_copy.wait()
    pl.semaphore_wait(barrier, len(peers))

    with jax.named_scope("gather"):
        for o in Z_ORDER:
            send(mine, mine, zs.at[o - 1], zr.at[o - 1], z_peer[o])
        for o in ALL_Z:
            block = xb.at[c, x, around(z, -o, NZ)]
            if o:
                arrived(block, zr.at[o - 1])
            for p in (2, 1, 3):
                send(block, block, xs.at[p - 1, o], xr.at[p - 1], x_peer[p])
        line = xb.at[c, x]
        send(line, line, cs.at[0], cr.at[0], sibling)
        for p in (1, 3, 2):
            line = xb.at[c, around(x, -p, NX)]
            arrived(line, xr.at[p - 1])
            send(line, line, cs.at[p], cr.at[p], sibling)
        for p in (0, 1, 3, 2):
            arrived(xb.at[1 - c, around(x, -p, NX)], cr.at[p])

    x2d[...] = xb[:, :, :, :, 0:DS].reshape(TOKENS, DS)
    ids = xb[:, :, :, :, DS:MSG].reshape(TOKENS, 128).astype(F32)
    first, second = ids[:, 0:1], ids[:, 1:2]

    with jax.named_scope("logits"):
        router_copy.wait()
        lg_own[...] = lax.dot_general(
            router_ref[...], x2d[...], (((1,), (1,)), ((), ())), preferred_element_type=F32)
        for p in range(1, NY):
            send(lg_own, lg_got.at[p - 1], ls.at[p - 1], lr.at[p - 1], y_peer[p])

    def gate_up(h):
        columns = slice(h * HCOL, (h + 1) * HCOL)
        for e in range(WINDOW):
            if h == 0:
                w_copies[2 * e].wait()
                w_copies[2 * e + 1].wait()
            both = jnp.concatenate([wg[e, :, columns], wu[e, :, columns]], axis=1)
            product = jnp.dot(x2d[...], both, preferred_element_type=F32)
            for k, named in enumerate((first, second)):
                before = yacc[h, k] if e else jnp.zeros((TOKENS, 2 * HCOL), F32)
                yacc[h, k] = jnp.where(named == float(e), product, before)

    def y_send(h):
        for q in range(NY):
            for k in range(2):
                ysend[h, q, k] = yacc[h, k, q * ROWS_Y:(q + 1) * ROWS_Y, :].astype(BF16)
        for p in (2, 1, 3):
            send(ysend.at[h, around(s, p, NY)], ygot.at[h, p - 1], ys.at[h, p - 1], yr.at[h, p - 1], y_peer[p])

    def activate(h):
        for p in (1, 3, 2):
            arrived(ygot.at[h, p - 1], yr.at[h, p - 1])
        for k in range(2):
            total = yacc[h, k, pl.ds(pl.multiple_of(s * ROWS_Y, ROWS_Y), ROWS_Y), :]
            for p in range(1, NY):
                total = total + ygot[h, p - 1, k].astype(F32)
            gate, up = total[:, :HCOL], total[:, HCOL:]
            hid[h, s, k] = (gate / (1.0 + jnp.exp(-gate)) * up).astype(BF16)
        block = hid.at[h, s]
        for p in (2, 1, 3):
            send(block, block, hs.at[h, p - 1], hr.at[h, p - 1], y_peer[p])

    with jax.named_scope("gate_up"):
        gate_up(0)
        y_send(0)
        gate_up(1)
        y_send(1)

    with jax.named_scope("shares"):
        logits = lg_own[...]
        for p in range(1, NY):
            arrived(lg_got.at[p - 1], lr.at[p - 1])
            logits = logits + lg_got[p - 1]
        logits = logits.T
        expert = lax.broadcasted_iota(jnp.int32, (TOKENS, EXPERTS), 1).astype(F32)
        a = jnp.sum(jnp.where(expert == first, logits, 0.0), axis=1, keepdims=True)
        b = jnp.sum(jnp.where(expert == second, logits, 0.0), axis=1, keepdims=True)
        share_first = 1.0 / (1.0 + jnp.exp(b - a))
        share_second = 1.0 / (1.0 + jnp.exp(a - b))

    with jax.named_scope("hidden"):
        activate(0)
        activate(1)
        for h in range(CHUNKS):
            for p in (1, 3, 2):
                arrived(hid.at[h, around(s, -p, NY)], hr.at[h, p - 1])
        for h in range(CHUNKS):
            h0 = hid[h, :, 0].reshape(TOKENS, HCOL).astype(F32)
            h1 = hid[h, :, 1].reshape(TOKENS, HCOL).astype(F32)
            for e in range(WINDOW):
                rows = jnp.where(first == float(e), h0, jnp.where(second == float(e), h1, 0.0))
                abuf[e, :, h * HCOL:(h + 1) * HCOL] = rows.astype(BF16)

    def down(n):
        for t in range(COLS // TILE):
            total = None
            for e in range(WINDOW):
                weight = jnp.where(first == float(e), share_first, 0.0)
                weight = weight + jnp.where(second == float(e), share_second, 0.0)
                start = n * COLS + t * TILE
                term = weight * jnp.dot(abuf[e], wd[e, :, start:start + TILE], preferred_element_type=F32)
                total = term if total is None else total + term
            pbuf[n, :, :, t * TILE:(t + 1) * TILE] = total.reshape(NC, CORE_ROWS, TILE)
        send(pbuf.at[n, 1 - c], f1got.at[n], f1s.at[n], f1r.at[n], sibling)

    def along_x(n):
        arrived(f1got.at[n], f1r.at[n])
        total = pbuf[n, c] + f1got[n]
        pbuf[n, c] = total
        for q in range(NX):
            f2send[n, q] = total[q * ROWS_X:(q + 1) * ROWS_X, :].astype(BF16)
        for p in (2, 1, 3):
            send(f2send.at[n, around(x, p, NX)], f2got.at[n, p - 1], f2s.at[n, p - 1], f2r.at[n, p - 1], x_peer[p])

    def along_z(n):
        total = pbuf[n, c, pl.ds(pl.multiple_of(x * ROWS_X, ROWS_X), ROWS_X), :]
        for p in (1, 3, 2):
            arrived(f2got.at[n, p - 1], f2r.at[n, p - 1])
            total = total + f2got[n, p - 1].astype(F32)
        total = total.reshape(NZ, TOK, COLS)
        f3own[n] = total
        f3send[n] = total.astype(BF16)
        for o in (4, 3, 5, 2, 6, 1, 7):
            send(f3send.at[n, around(z, o, NZ)], f3got.at[n, o - 1],
                 f3s.at[n, o - 1], f3r.at[n, o - 1], z_peer[o])

    with jax.named_scope("down"):
        for e in range(WINDOW):
            w_copies[2 * WINDOW + e].wait()
        down(0)
        down(1)
        along_x(0)
        down(2)
        along_x(1)
        along_x(2)

    with jax.named_scope("along_z"):
        for n in range(PARTS):
            along_z(n)
        for n in range(PARTS):
            total = f3own[n, z]
            for o in Z_ORDER:
                arrived(f3got.at[n, o - 1], f3r.at[n, o - 1])
                total = total + f3got[n, o - 1].astype(F32)
            out_ref[:, n * COLS:(n + 1) * COLS] = total.astype(BF16)

    for cp in sent:
        cp.wait_send()


def body(tokens, expert_ids, router, w_gate, w_up, w_down):
    vmem, hbm = pl.BlockSpec(memory_space=pltpu.VMEM), pl.BlockSpec(memory_space=pl.ANY)
    dma = pltpu.SemaphoreType.DMA
    scratch = [
        pltpu.VMEM((NC, NX, NZ, TOK, MSG), BF16),
        pltpu.VMEM((TOKENS, DS), BF16),
        pltpu.VMEM((WINDOW, DS, HID), BF16),
        pltpu.VMEM((WINDOW, DS, HID), BF16),
        pltpu.VMEM((WINDOW, HID, DS), BF16),
        pltpu.VMEM((EXPERTS, DS), BF16),
        pltpu.SMEM((2, TOK), jnp.int32),
        pltpu.VMEM((EXPERTS, TOKENS), F32),
        pltpu.VMEM((NY - 1, EXPERTS, TOKENS), F32),
        pltpu.VMEM((CHUNKS, 2, TOKENS, 2 * HCOL), F32),
        pltpu.VMEM((CHUNKS, NY, 2, ROWS_Y, 2 * HCOL), BF16),
        pltpu.VMEM((CHUNKS, NY - 1, 2, ROWS_Y, 2 * HCOL), BF16),
        pltpu.VMEM((CHUNKS, NY, 2, ROWS_Y, HCOL), BF16),
        pltpu.VMEM((WINDOW, TOKENS, HID), BF16),
        pltpu.VMEM((PARTS, NC, CORE_ROWS, COLS), F32),
        pltpu.VMEM((PARTS, CORE_ROWS, COLS), F32),
        pltpu.VMEM((PARTS, NX, ROWS_X, COLS), BF16),
        pltpu.VMEM((PARTS, NX - 1, ROWS_X, COLS), BF16),
        pltpu.VMEM((PARTS, NZ, TOK, COLS), F32),
        pltpu.VMEM((PARTS, NZ, TOK, COLS), BF16),
        pltpu.VMEM((PARTS, NZ - 1, TOK, COLS), BF16),
        dma, dma, dma, dma((3, WINDOW)),
        dma((NZ - 1,)), dma((NZ - 1,)),
        dma((NX - 1, NZ)), dma((NX - 1,)),
        dma((NX,)), dma((NX,)),
        dma((NY - 1,)), dma((NY - 1,)),
        dma((CHUNKS, NY - 1)), dma((CHUNKS, NY - 1)),
        dma((CHUNKS, NY - 1)), dma((CHUNKS, NY - 1)),
        dma((PARTS,)), dma((PARTS,)),
        dma((PARTS, NX - 1)), dma((PARTS, NX - 1)),
        dma((PARTS, NZ - 1)), dma((PARTS, NZ - 1)),
    ]
    flops = 6 * WINDOW * TOKENS * DS * HID
    return pl.pallas_call(
        kernel,
        out_shape=jax.ShapeDtypeStruct((TOK, DS), BF16),
        in_specs=[hbm] * 6,
        out_specs=vmem,
        scratch_shapes=scratch,
        compiler_params=pltpu.CompilerParams(
            collective_id=0, has_side_effects=True, vmem_limit_bytes=60 * 1024 * 1024),
        cost_estimate=pl.CostEstimate(flops=flops, bytes_accessed=6 * WINDOW * DS * HID, transcendentals=0),
    )(tokens, expert_ids.T, router.T, w_gate, w_up, w_down)


def solution(mesh):
    placed = (
        P("dp", "seq"),
        P("dp", None),
        P("seq", None),
        P(None, "seq", "dp"),
        P(None, "seq", "dp"),
        P(None, "dp", "seq"),
    )
    return jax.shard_map(
        body, mesh=mesh, in_specs=placed, out_specs=P("dp", "seq"), check_vma=False
    )
```

```python
import functools

import jax
import jax.numpy as jnp
from jax import lax
from jax.experimental import pallas as pl
from jax.experimental.pallas import tpu as pltpu
from jax.sharding import PartitionSpec as P

NX, NZ, NC, NY = 4, 8, 2, 4
EXPERTS = 8
WINDOW = 5
TOK = 4
TOKENS = TOK * NX * NZ * NC
CORE_ROWS = TOKENS // NC
DS = 1536
HID = 256
CHUNKS = 2
PARTS = 3
COLS = DS // PARTS
TILE = 256
MSG = DS + 128
ROWS_Y = CORE_ROWS // NY
ROWS_X = CORE_ROWS // NX
Z_ORDER = (1, 7, 2, 6, 3, 5, 4)
ALL_Z = (0, *Z_ORDER)
F32, BF16 = jnp.float32, jnp.bfloat16


def kernel(
    tokens_ref, ids_hbm, router_hbm, wg_ref, wu_ref, wd_ref, out_ref,
    xb, x2d, wg, wu, wd, router_ref, ids_ref, lg_own, lg_got, yacc, ysend, ygot, hid, abuf,
    pbuf, f1got, f2send, f2got, f3own, f3send, f3got,
    tok_sem, id_sem, router_sem, w_sem, zs, zr, xs, xr, cs, cr, ks, kr, ls, lr, ys, yr, hs, hr,
    f1s, f1r, f2s, f2r, f3s, f3r,
):
    d, s = lax.axis_index("dp"), lax.axis_index("seq")
    c = lax.rem(d, NC)
    z = lax.rem(lax.div(d, NC), NZ)
    x = lax.div(d, NC * NZ)

    def dev(px, pz, pc, ps):
        return ((px * NZ + pz) * NC + pc, ps)

    def around(v, o, n):
        return lax.rem(v + (o + n), n)

    sibling = dev(x, z, 1 - c, s)
    z_peer = {o: dev(x, around(z, o, NZ), c, s) for o in range(1, NZ)}
    z_cross = {o: dev(x, around(z, o, NZ), 1 - c, s) for o in range(NZ)}
    x_peer = {o: dev(around(x, o, NX), z, c, s) for o in range(1, NX)}
    y_peer = {o: dev(x, z, c, around(s, o, NY)) for o in range(1, NY)}
    peers = [*z_cross.values(), *z_peer.values(), *x_peer.values(), *y_peer.values()]
    sent = []

    core_of = (1 - c, c)

    def send(src, dst, ssem, rsem, to):
        cp = pltpu.make_async_remote_copy(
            src_ref=src, dst_ref=dst, send_sem=ssem, recv_sem=rsem,
            device_id=to, device_id_type=pl.DeviceIdType.MESH)
        cp.start()
        sent.append(cp)

    def arrived(dst, rsem):
        pltpu.make_async_remote_copy(
            src_ref=dst, dst_ref=dst, send_sem=rsem, recv_sem=rsem,
            device_id=sibling, device_id_type=pl.DeviceIdType.MESH).wait_recv()

    barrier = pltpu.get_barrier_semaphore()
    for peer in peers:
        pl.semaphore_signal(barrier, inc=1, device_id=peer, device_id_type=pl.DeviceIdType.MESH)

    mine = xb.at[c, x, z]
    id_copy = pltpu.make_async_copy(ids_hbm, ids_ref, id_sem)
    tok_copy = pltpu.make_async_copy(tokens_ref, mine.at[:, pl.ds(0, DS)], tok_sem)
    router_copy = pltpu.make_async_copy(router_hbm, router_ref, router_sem)
    w_copies = []
    for e in range(WINDOW):
        for i, (src, dst) in enumerate(((wg_ref, wg), (wu_ref, wu))):
            w_copies.append(pltpu.make_async_copy(src.at[e], dst.at[e], w_sem.at[i, e]))
    for e in range(WINDOW):
        w_copies.append(pltpu.make_async_copy(wd_ref.at[e], wd.at[e], w_sem.at[2, e]))
    for cp in (id_copy, tok_copy, router_copy, *w_copies):
        cp.start()

    id_copy.wait()
    row = lax.broadcasted_iota(jnp.int32, (TOK, 128), 0)
    lane = lax.broadcasted_iota(jnp.int32, (TOK, 128), 1)
    named = jnp.zeros((TOK, 128), jnp.int32)
    for t in range(TOK):
        for k in range(2):
            named = jnp.where((row == t) & (lane == k), ids_ref[k, t], named)
    xb[c, x, z, :, DS:MSG] = named.astype(F32).astype(BF16)
    tok_copy.wait()
    pl.semaphore_wait(barrier, len(peers))

    with jax.named_scope("gather"):
        for o in ALL_Z:
            send(mine, mine, zs.at[o], zr.at[o], z_cross[o])
        for o in ALL_Z:
            block = xb.at[1 - c, x, around(z, -o, NZ)]
            arrived(block, zr.at[o])
            for p in (1, 3, 2):
                send(block, block, xs.at[p - 1, o], xr.at[p - 1], x_peer[p])
            if o:
                send(block, block, cs.at[o - 1], cr.at[o - 1], sibling)
        for p in (1, 3, 2):
            line = xb.at[1 - c, around(x, -p, NX)]
            arrived(line, xr.at[p - 1])
            send(line, line, ks.at[p - 1], kr.at[p - 1], sibling)

    first, second = [None] * CHUNKS, [None] * CHUNKS

    def take_rows(h):
        cores = core_of[h]
        x2d[cores] = xb[cores, :, :, :, 0:DS].reshape(CORE_ROWS, DS)
        ids = xb[cores, :, :, :, DS:MSG].reshape(CORE_ROWS, 128).astype(F32)
        first[h], second[h] = ids[:, 0:1], ids[:, 1:2]

    def gate_up(h):
        for e in range(WINDOW):
            for i, w in enumerate((wg, wu)):
                if h == 0:
                    w_copies[2 * e + i].wait()
                product = jnp.dot(x2d[core_of[h]], w[e], preferred_element_type=F32)
                columns = slice(i * HID, (i + 1) * HID)
                for k, named in enumerate((first[h], second[h])):
                    before = yacc[h, k, :, columns] if e else jnp.zeros((CORE_ROWS, HID), F32)
                    yacc[h, k, :, columns] = jnp.where(named == float(e), product, before)

    def y_send(h):
        for q in range(NY):
            for k in range(2):
                ysend[h, q, k] = yacc[h, k, q * ROWS_Y:(q + 1) * ROWS_Y, :].astype(BF16)
        for p in (2, 1, 3):
            send(ysend.at[h, around(s, p, NY)], ygot.at[h, p - 1], ys.at[h, p - 1], yr.at[h, p - 1], y_peer[p])

    def activate(h):
        for p in (1, 3, 2):
            arrived(ygot.at[h, p - 1], yr.at[h, p - 1])
        for k in range(2):
            total = yacc[h, k, pl.ds(pl.multiple_of(s * ROWS_Y, ROWS_Y), ROWS_Y), :]
            for p in range(1, NY):
                total = total + ygot[h, p - 1, k].astype(F32)
            gate, up = total[:, :HID], total[:, HID:]
            hid[core_of[h], s, k] = (gate / (1.0 + jnp.exp(-gate)) * up).astype(BF16)
        block = hid.at[core_of[h], s]
        for p in (2, 1, 3):
            send(block, block, hs.at[h, p - 1], hr.at[h, p - 1], y_peer[p])

    with jax.named_scope("gate_up"):
        take_rows(0)
        gate_up(0)
        y_send(0)
        for o in Z_ORDER:
            arrived(xb.at[c, x, around(z, -o, NZ)], cr.at[o - 1])
        for p in (1, 3, 2):
            arrived(xb.at[c, around(x, -p, NX)], kr.at[p - 1])
        take_rows(1)
        gate_up(1)
        y_send(1)

    weights = []
    with jax.named_scope("shares"):
        router_copy.wait()
        for i in range(NC):
            lg_own[i] = lax.dot_general(
                router_ref[...], x2d[i], (((1,), (1,)), ((), ())), preferred_element_type=F32)
        for p in range(1, NY):
            send(lg_own, lg_got.at[p - 1], ls.at[p - 1], lr.at[p - 1], y_peer[p])
        activate(0)
        for p in range(1, NY):
            arrived(lg_got.at[p - 1], lr.at[p - 1])
        expert = lax.broadcasted_iota(jnp.int32, (CORE_ROWS, EXPERTS), 1).astype(F32)
        for h in range(CHUNKS):
            logits = lg_own[core_of[h]]
            for p in range(1, NY):
                logits = logits + lg_got[p - 1, core_of[h]]
            logits = logits.T
            a = jnp.sum(jnp.where(expert == first[h], logits, 0.0), axis=1, keepdims=True)
            b = jnp.sum(jnp.where(expert == second[h], logits, 0.0), axis=1, keepdims=True)
            share_first = 1.0 / (1.0 + jnp.exp(b - a))
            share_second = 1.0 / (1.0 + jnp.exp(a - b))
            weights.append([
                jnp.where(first[h] == float(e), share_first, 0.0)
                + jnp.where(second[h] == float(e), share_second, 0.0) for e in range(WINDOW)])

    def collect(h):
        for p in (1, 3, 2):
            arrived(hid.at[core_of[h], around(s, -p, NY)], hr.at[h, p - 1])
        h0 = hid[core_of[h], :, 0].reshape(CORE_ROWS, HID).astype(F32)
        h1 = hid[core_of[h], :, 1].reshape(CORE_ROWS, HID).astype(F32)
        for e in range(WINDOW):
            rows = jnp.where(first[h] == float(e), h0, jnp.where(second[h] == float(e), h1, 0.0))
            abuf[h, e] = rows.astype(BF16)

    def down(h, n):
        for t in range(COLS // TILE):
            total = None
            for e in range(WINDOW):
                start = n * COLS + t * TILE
                term = weights[h][e] * jnp.dot(
                    abuf[h, e], wd[e, :, start:start + TILE], preferred_element_type=F32)
                total = term if total is None else total + term
            pbuf[n, core_of[h], :, t * TILE:(t + 1) * TILE] = total
        if h == 0:
            send(pbuf.at[n, 1 - c], f1got.at[n], f1s.at[n], f1r.at[n], sibling)

    def along_x(n):
        arrived(f1got.at[n], f1r.at[n])
        total = pbuf[n, c] + f1got[n]
        pbuf[n, c] = total
        for q in range(NX):
            f2send[n, q] = total[q * ROWS_X:(q + 1) * ROWS_X, :].astype(BF16)
        for p in (2, 1, 3):
            send(f2send.at[n, around(x, p, NX)], f2got.at[n, p - 1], f2s.at[n, p - 1], f2r.at[n, p - 1], x_peer[p])

    def along_z(n):
        total = pbuf[n, c, pl.ds(pl.multiple_of(x * ROWS_X, ROWS_X), ROWS_X), :]
        for p in (1, 3, 2):
            arrived(f2got.at[n, p - 1], f2r.at[n, p - 1])
            total = total + f2got[n, p - 1].astype(F32)
        total = total.reshape(NZ, TOK, COLS)
        f3own[n] = total
        f3send[n] = total.astype(BF16)
        for o in (4, 3, 5, 2, 6, 1, 7):
            send(f3send.at[n, around(z, o, NZ)], f3got.at[n, o - 1],
                 f3s.at[n, o - 1], f3r.at[n, o - 1], z_peer[o])

    with jax.named_scope("down"):
        activate(1)
        for e in range(WINDOW):
            w_copies[2 * WINDOW + e].wait()
        collect(0)
        for n in range(PARTS):
            down(0, n)
    with jax.named_scope("down_own"):
        collect(1)
        for n in range(PARTS):
            down(1, n)
            along_x(n)

    with jax.named_scope("along_z"):
        for n in range(PARTS):
            along_z(n)
        for n in range(PARTS):
            total = f3own[n, z]
            for o in Z_ORDER:
                arrived(f3got.at[n, o - 1], f3r.at[n, o - 1])
                total = total + f3got[n, o - 1].astype(F32)
            out_ref[:, n * COLS:(n + 1) * COLS] = total.astype(BF16)

    for cp in sent:
        cp.wait_send()


def body(tokens, expert_ids, router, w_gate, w_up, w_down):
    vmem, hbm = pl.BlockSpec(memory_space=pltpu.VMEM), pl.BlockSpec(memory_space=pl.ANY)
    dma = pltpu.SemaphoreType.DMA
    scratch = [
        pltpu.VMEM((NC, NX, NZ, TOK, MSG), BF16),
        pltpu.VMEM((NC, CORE_ROWS, DS), BF16),
        pltpu.VMEM((WINDOW, DS, HID), BF16),
        pltpu.VMEM((WINDOW, DS, HID), BF16),
        pltpu.VMEM((WINDOW, HID, DS), BF16),
        pltpu.VMEM((EXPERTS, DS), BF16),
        pltpu.SMEM((2, TOK), jnp.int32),
        pltpu.VMEM((NC, EXPERTS, CORE_ROWS), F32),
        pltpu.VMEM((NY - 1, NC, EXPERTS, CORE_ROWS), F32),
        pltpu.VMEM((CHUNKS, 2, CORE_ROWS, 2 * HID), F32),
        pltpu.VMEM((CHUNKS, NY, 2, ROWS_Y, 2 * HID), BF16),
        pltpu.VMEM((CHUNKS, NY - 1, 2, ROWS_Y, 2 * HID), BF16),
        pltpu.VMEM((NC, NY, 2, ROWS_Y, HID), BF16),
        pltpu.VMEM((CHUNKS, WINDOW, CORE_ROWS, HID), BF16),
        pltpu.VMEM((PARTS, NC, CORE_ROWS, COLS), F32),
        pltpu.VMEM((PARTS, CORE_ROWS, COLS), F32),
        pltpu.VMEM((PARTS, NX, ROWS_X, COLS), BF16),
        pltpu.VMEM((PARTS, NX - 1, ROWS_X, COLS), BF16),
        pltpu.VMEM((PARTS, NZ, TOK, COLS), F32),
        pltpu.VMEM((PARTS, NZ, TOK, COLS), BF16),
        pltpu.VMEM((PARTS, NZ - 1, TOK, COLS), BF16),
        dma, dma, dma, dma((3, WINDOW)),
        dma((NZ,)), dma((NZ,)),
        dma((NX - 1, NZ)), dma((NX - 1,)),
        dma((NZ - 1,)), dma((NZ - 1,)),
        dma((NX - 1,)), dma((NX - 1,)),
        dma((NY - 1,)), dma((NY - 1,)),
        dma((CHUNKS, NY - 1)), dma((CHUNKS, NY - 1)),
        dma((CHUNKS, NY - 1)), dma((CHUNKS, NY - 1)),
        dma((PARTS,)), dma((PARTS,)),
        dma((PARTS, NX - 1)), dma((PARTS, NX - 1)),
        dma((PARTS, NZ - 1)), dma((PARTS, NZ - 1)),
    ]
    flops = 6 * WINDOW * TOKENS * DS * HID
    return pl.pallas_call(
        kernel,
        out_shape=jax.ShapeDtypeStruct((TOK, DS), BF16),
        in_specs=[hbm] * 6,
        out_specs=vmem,
        scratch_shapes=scratch,
        compiler_params=pltpu.CompilerParams(
            collective_id=0, has_side_effects=True, vmem_limit_bytes=60 * 1024 * 1024),
        cost_estimate=pl.CostEstimate(flops=flops, bytes_accessed=6 * WINDOW * DS * HID, transcendentals=0),
    )(tokens, expert_ids.T, router.T, w_gate, w_up, w_down)


def solution(mesh):
    placed = (
        P("dp", "seq"),
        P("dp", None),
        P("seq", None),
        P(None, "seq", "dp"),
        P(None, "seq", "dp"),
        P(None, "dp", "seq"),
    )
    return jax.shard_map(
        body, mesh=mesh, in_specs=placed, out_specs=P("dp", "seq"), check_vma=False
    )
```

```python
import functools

import jax
import jax.numpy as jnp
from jax import lax
from jax.experimental import pallas as pl
from jax.experimental.pallas import tpu as pltpu
from jax.sharding import PartitionSpec as P

NX, NZ, NC, NY = 4, 8, 2, 4
EXPERTS = 8
WINDOW = 5
TOK = 4
TOKENS = TOK * NX * NZ * NC
CORE_ROWS = TOKENS // NC
DS = 1536
HID = 256
CHUNKS = 2
PARTS = 3
COLS = DS // PARTS
TILE = 256
MSG = DS + 128
ROWS_Y = CORE_ROWS // NY
ROWS_X = CORE_ROWS // NX
Z_ORDER = (1, 7, 2, 6, 3, 5, 4)
ALL_Z = (0, *Z_ORDER)
F32, BF16 = jnp.float32, jnp.bfloat16


def kernel(
    tokens_ref, ids_hbm, router_hbm, wg_ref, wu_ref, wd_ref, out_ref,
    xb, x2d, wg, wu, wd, router_ref, ids_ref, lg_own, lg_got, yacc, ysend, ygot, hid, abuf,
    pbuf, f1got, f2send, f2got, f3own, f3send, f3got,
    tok_sem, id_sem, router_sem, w_sem, zs, zr, xs, xr, cs, cr, ks, kr, ls, lr, ys, yr, hs, hr,
    f1s, f1r, f2s, f2r, f3s, f3r,
):
    d, s = lax.axis_index("dp"), lax.axis_index("seq")
    c = lax.rem(d, NC)
    z = lax.rem(lax.div(d, NC), NZ)
    x = lax.div(d, NC * NZ)

    def dev(px, pz, pc, ps):
        return ((px * NZ + pz) * NC + pc, ps)

    def around(v, o, n):
        return lax.rem(v + (o + n), n)

    sibling = dev(x, z, 1 - c, s)
    z_peer = {o: dev(x, around(z, o, NZ), c, s) for o in range(1, NZ)}
    z_cross = {o: dev(x, around(z, o, NZ), 1 - c, s) for o in range(NZ)}
    x_peer = {o: dev(around(x, o, NX), z, c, s) for o in range(1, NX)}
    y_peer = {o: dev(x, z, c, around(s, o, NY)) for o in range(1, NY)}
    peers = [*z_cross.values(), *z_peer.values(), *x_peer.values(), *y_peer.values()]
    sent = []

    core_of = (1 - c, c)

    def send(src, dst, ssem, rsem, to):
        cp = pltpu.make_async_remote_copy(
            src_ref=src, dst_ref=dst, send_sem=ssem, recv_sem=rsem,
            device_id=to, device_id_type=pl.DeviceIdType.MESH)
        cp.start()
        sent.append(cp)

    def arrived(dst, rsem):
        pltpu.make_async_remote_copy(
            src_ref=dst, dst_ref=dst, send_sem=rsem, recv_sem=rsem,
            device_id=sibling, device_id_type=pl.DeviceIdType.MESH).wait_recv()

    barrier = pltpu.get_barrier_semaphore()
    for peer in peers:
        pl.semaphore_signal(barrier, inc=1, device_id=peer, device_id_type=pl.DeviceIdType.MESH)

    mine = xb.at[c, x, z]
    id_copy = pltpu.make_async_copy(ids_hbm, ids_ref, id_sem)
    tok_copy = pltpu.make_async_copy(tokens_ref, mine.at[:, pl.ds(0, DS)], tok_sem)
    router_copy = pltpu.make_async_copy(router_hbm, router_ref, router_sem)
    w_copies = []
    for e in range(WINDOW):
        for i, (src, dst) in enumerate(((wg_ref, wg), (wu_ref, wu))):
            w_copies.append(pltpu.make_async_copy(src.at[e], dst.at[e], w_sem.at[i, e]))
    for e in range(WINDOW):
        w_copies.append(pltpu.make_async_copy(wd_ref.at[e], wd.at[e], w_sem.at[2, e]))
    for cp in (id_copy, tok_copy, router_copy, *w_copies):
        cp.start()

    id_copy.wait()
    row = lax.broadcasted_iota(jnp.int32, (TOK, 128), 0)
    lane = lax.broadcasted_iota(jnp.int32, (TOK, 128), 1)
    named = jnp.zeros((TOK, 128), jnp.int32)
    for t in range(TOK):
        for k in range(2):
            named = jnp.where((row == t) & (lane == k), ids_ref[k, t], named)
    xb[c, x, z, :, DS:MSG] = named.astype(F32).astype(BF16)
    tok_copy.wait()
    pl.semaphore_wait(barrier, len(peers))

    with jax.named_scope("gather"):
        for o in ALL_Z:
            send(mine, mine, zs.at[o], zr.at[o], z_cross[o])
        for o in ALL_Z:
            block = xb.at[1 - c, x, around(z, -o, NZ)]
            arrived(block, zr.at[o])
            for p in (1, 3, 2):
                send(block, block, xs.at[p - 1, o], xr.at[p - 1], x_peer[p])
            if o:
                send(block, block, cs.at[o - 1], cr.at[o - 1], sibling)
        for p in (1, 3, 2):
            line = xb.at[1 - c, around(x, -p, NX)]
            arrived(line, xr.at[p - 1])
            send(line, line, ks.at[p - 1], kr.at[p - 1], sibling)

    first, second = [None] * CHUNKS, [None] * CHUNKS

    def take_rows(h):
        cores = core_of[h]
        x2d[cores] = xb[cores, :, :, :, 0:DS].reshape(CORE_ROWS, DS)
        ids = xb[cores, :, :, :, DS:MSG].reshape(CORE_ROWS, 128).astype(F32)
        first[h], second[h] = ids[:, 0:1], ids[:, 1:2]

    def gate_up(h):
        for e in range(WINDOW):
            for i, w in enumerate((wg, wu)):
                if h == 0:
                    w_copies[2 * e + i].wait()
                product = jnp.dot(x2d[core_of[h]], w[e], preferred_element_type=F32)
                columns = slice(i * HID, (i + 1) * HID)
                for k, named in enumerate((first[h], second[h])):
                    before = yacc[h, k, :, columns] if e else jnp.zeros((CORE_ROWS, HID), F32)
                    yacc[h, k, :, columns] = jnp.where(named == float(e), product, before)

    def y_send(h):
        for q in range(NY):
            for k in range(2):
                ysend[h, q, k] = yacc[h, k, q * ROWS_Y:(q + 1) * ROWS_Y, :].astype(BF16)
        for p in (2, 1, 3):
            send(ysend.at[h, around(s, p, NY)], ygot.at[h, p - 1], ys.at[h, p - 1], yr.at[h, p - 1], y_peer[p])

    def activate(h):
        for p in (1, 3, 2):
            arrived(ygot.at[h, p - 1], yr.at[h, p - 1])
        for k in range(2):
            total = yacc[h, k, pl.ds(pl.multiple_of(s * ROWS_Y, ROWS_Y), ROWS_Y), :]
            for p in range(1, NY):
                total = total + ygot[h, p - 1, k].astype(F32)
            gate, up = total[:, :HID], total[:, HID:]
            hid[core_of[h], s, k] = (gate / (1.0 + jnp.exp(-gate)) * up).astype(BF16)
        block = hid.at[core_of[h], s]
        for p in (2, 1, 3):
            send(block, block, hs.at[h, p - 1], hr.at[h, p - 1], y_peer[p])

    with jax.named_scope("gate_up"):
        take_rows(0)
        gate_up(0)
        y_send(0)
        for o in Z_ORDER:
            arrived(xb.at[c, x, around(z, -o, NZ)], cr.at[o - 1])
        for p in (1, 3, 2):
            arrived(xb.at[c, around(x, -p, NX)], kr.at[p - 1])
        take_rows(1)
        gate_up(1)
        y_send(1)

    weights = []
    with jax.named_scope("shares"):
        router_copy.wait()
        for i in range(NC):
            lg_own[i] = lax.dot_general(
                router_ref[...], x2d[i], (((1,), (1,)), ((), ())), preferred_element_type=F32)
        for p in range(1, NY):
            send(lg_own, lg_got.at[p - 1], ls.at[p - 1], lr.at[p - 1], y_peer[p])
        activate(0)
        activate(1)
        for p in range(1, NY):
            arrived(lg_got.at[p - 1], lr.at[p - 1])
        expert = lax.broadcasted_iota(jnp.int32, (CORE_ROWS, EXPERTS), 1).astype(F32)
        for h in range(CHUNKS):
            logits = lg_own[core_of[h]]
            for p in range(1, NY):
                logits = logits + lg_got[p - 1, core_of[h]]
            logits = logits.T
            a = jnp.sum(jnp.where(expert == first[h], logits, 0.0), axis=1, keepdims=True)
            b = jnp.sum(jnp.where(expert == second[h], logits, 0.0), axis=1, keepdims=True)
            share_first = 1.0 / (1.0 + jnp.exp(b - a))
            share_second = 1.0 / (1.0 + jnp.exp(a - b))
            weights.append([
                jnp.where(first[h] == float(e), share_first, 0.0)
                + jnp.where(second[h] == float(e), share_second, 0.0) for e in range(WINDOW)])

    def collect(h):
        for p in (1, 3, 2):
            arrived(hid.at[core_of[h], around(s, -p, NY)], hr.at[h, p - 1])
        h0 = hid[core_of[h], :, 0].reshape(CORE_ROWS, HID).astype(F32)
        h1 = hid[core_of[h], :, 1].reshape(CORE_ROWS, HID).astype(F32)
        for e in range(WINDOW):
            rows = jnp.where(first[h] == float(e), h0, jnp.where(second[h] == float(e), h1, 0.0))
            abuf[h, e] = rows.astype(BF16)

    def down(h, n):
        for t in range(COLS // TILE):
            total = None
            for e in range(WINDOW):
                start = n * COLS + t * TILE
                term = weights[h][e] * jnp.dot(
                    abuf[h, e], wd[e, :, start:start + TILE], preferred_element_type=F32)
                total = term if total is None else total + term
            pbuf[n, core_of[h], :, t * TILE:(t + 1) * TILE] = total
        if h == 0:
            send(pbuf.at[n, 1 - c], f1got.at[n], f1s.at[n], f1r.at[n], sibling)

    def along_x(n):
        arrived(f1got.at[n], f1r.at[n])
        total = pbuf[n, c] + f1got[n]
        pbuf[n, c] = total
        for q in range(NX):
            f2send[n, q] = total[q * ROWS_X:(q + 1) * ROWS_X, :].astype(BF16)
        for p in (1, 3, 2):
            send(f2send.at[n, around(x, p, NX)], f2got.at[n, p - 1], f2s.at[n, p - 1], f2r.at[n, p - 1], x_peer[p])

    def along_z(n):
        total = pbuf[n, c, pl.ds(pl.multiple_of(x * ROWS_X, ROWS_X), ROWS_X), :]
        for p in (1, 3, 2):
            arrived(f2got.at[n, p - 1], f2r.at[n, p - 1])
            total = total + f2got[n, p - 1].astype(F32)
        total = total.reshape(NZ, TOK, COLS)
        f3own[n] = total
        f3send[n] = total.astype(BF16)
        for o in (4, 3, 5, 2, 6, 1, 7):
            send(f3send.at[n, around(z, o, NZ)], f3got.at[n, o - 1],
                 f3s.at[n, o - 1], f3r.at[n, o - 1], z_peer[o])

    with jax.named_scope("down"):
        for e in range(WINDOW):
            w_copies[2 * WINDOW + e].wait()
        collect(0)
        for n in range(PARTS):
            down(0, n)
    with jax.named_scope("down_own"):
        collect(1)
        for n in range(PARTS):
            down(1, n)
            along_x(n)

    with jax.named_scope("along_z"):
        for n in range(PARTS):
            along_z(n)
        for n in range(PARTS):
            total = f3own[n, z]
            for o in Z_ORDER:
                arrived(f3got.at[n, o - 1], f3r.at[n, o - 1])
                total = total + f3got[n, o - 1].astype(F32)
            out_ref[:, n * COLS:(n + 1) * COLS] = total.astype(BF16)

    for cp in sent:
        cp.wait_send()


def body(tokens, expert_ids, router, w_gate, w_up, w_down):
    vmem, hbm = pl.BlockSpec(memory_space=pltpu.VMEM), pl.BlockSpec(memory_space=pl.ANY)
    dma = pltpu.SemaphoreType.DMA
    scratch = [
        pltpu.VMEM((NC, NX, NZ, TOK, MSG), BF16),
        pltpu.VMEM((NC, CORE_ROWS, DS), BF16),
        pltpu.VMEM((WINDOW, DS, HID), BF16),
        pltpu.VMEM((WINDOW, DS, HID), BF16),
        pltpu.VMEM((WINDOW, HID, DS), BF16),
        pltpu.VMEM((EXPERTS, DS), BF16),
        pltpu.SMEM((2, TOK), jnp.int32),
        pltpu.VMEM((NC, EXPERTS, CORE_ROWS), F32),
        pltpu.VMEM((NY - 1, NC, EXPERTS, CORE_ROWS), F32),
        pltpu.VMEM((CHUNKS, 2, CORE_ROWS, 2 * HID), F32),
        pltpu.VMEM((CHUNKS, NY, 2, ROWS_Y, 2 * HID), BF16),
        pltpu.VMEM((CHUNKS, NY - 1, 2, ROWS_Y, 2 * HID), BF16),
        pltpu.VMEM((NC, NY, 2, ROWS_Y, HID), BF16),
        pltpu.VMEM((CHUNKS, WINDOW, CORE_ROWS, HID), BF16),
        pltpu.VMEM((PARTS, NC, CORE_ROWS, COLS), F32),
        pltpu.VMEM((PARTS, CORE_ROWS, COLS), F32),
        pltpu.VMEM((PARTS, NX, ROWS_X, COLS), BF16),
        pltpu.VMEM((PARTS, NX - 1, ROWS_X, COLS), BF16),
        pltpu.VMEM((PARTS, NZ, TOK, COLS), F32),
        pltpu.VMEM((PARTS, NZ, TOK, COLS), BF16),
        pltpu.VMEM((PARTS, NZ - 1, TOK, COLS), BF16),
        dma, dma, dma, dma((3, WINDOW)),
        dma((NZ,)), dma((NZ,)),
        dma((NX - 1, NZ)), dma((NX - 1,)),
        dma((NZ - 1,)), dma((NZ - 1,)),
        dma((NX - 1,)), dma((NX - 1,)),
        dma((NY - 1,)), dma((NY - 1,)),
        dma((CHUNKS, NY - 1)), dma((CHUNKS, NY - 1)),
        dma((CHUNKS, NY - 1)), dma((CHUNKS, NY - 1)),
        dma((PARTS,)), dma((PARTS,)),
        dma((PARTS, NX - 1)), dma((PARTS, NX - 1)),
        dma((PARTS, NZ - 1)), dma((PARTS, NZ - 1)),
    ]
    flops = 6 * WINDOW * TOKENS * DS * HID
    return pl.pallas_call(
        kernel,
        out_shape=jax.ShapeDtypeStruct((TOK, DS), BF16),
        in_specs=[hbm] * 6,
        out_specs=vmem,
        scratch_shapes=scratch,
        compiler_params=pltpu.CompilerParams(
            collective_id=0, has_side_effects=True, vmem_limit_bytes=60 * 1024 * 1024),
        cost_estimate=pl.CostEstimate(flops=flops, bytes_accessed=6 * WINDOW * DS * HID, transcendentals=0),
    )(tokens, expert_ids.T, router.T, w_gate, w_up, w_down)


def solution(mesh):
    placed = (
        P("dp", "seq"),
        P("dp", None),
        P("seq", None),
        P(None, "seq", "dp"),
        P(None, "seq", "dp"),
        P(None, "dp", "seq"),
    )
    return jax.shard_map(
        body, mesh=mesh, in_specs=placed, out_specs=P("dp", "seq"), check_vma=False
    )
```

```python
import functools

import jax
import jax.numpy as jnp
from jax import lax
from jax.experimental import pallas as pl
from jax.experimental.pallas import tpu as pltpu
from jax.sharding import PartitionSpec as P

NX, NZ, NC, NY = 4, 8, 2, 4
EXPERTS = 8
WINDOW = 5
TOK = 4
TOKENS = TOK * NX * NZ * NC
CORE_ROWS = TOKENS // NC
DS = 1536
HID = 256
CHUNKS = 2
PARTS = 3
COLS = DS // PARTS
TILE = 256
MSG = DS + 128
ROWS_Y = CORE_ROWS // NY
ROWS_X = CORE_ROWS // NX
Z_ORDER = (1, 7, 2, 6, 3, 5, 4)
ALL_Z = (0, *Z_ORDER)
F32, BF16 = jnp.float32, jnp.bfloat16


def kernel(
    tokens_ref, ids_hbm, router_hbm, wg_ref, wu_ref, wd_ref, out_ref,
    xb, x2d, wg, wu, wd, router_ref, ids_ref, lg_own, lg_got, yacc, ysend, ygot, hid, abuf,
    pbuf, f1got, f2send, f2got, f3own, f3send, f3got,
    tok_sem, id_sem, router_sem, w_sem, zs, zr, xs, xr, cs, cr, ks, kr, ls, lr, ys, yr, hs, hr,
    f1s, f1r, f2s, f2r, f3s, f3r,
):
    d, s = lax.axis_index("dp"), lax.axis_index("seq")
    c = lax.rem(d, NC)
    z = lax.rem(lax.div(d, NC), NZ)
    x = lax.div(d, NC * NZ)

    def dev(px, pz, pc, ps):
        return ((px * NZ + pz) * NC + pc, ps)

    def around(v, o, n):
        return lax.rem(v + (o + n), n)

    sibling = dev(x, z, 1 - c, s)
    z_peer = {o: dev(x, around(z, o, NZ), c, s) for o in range(1, NZ)}
    z_cross = {o: dev(x, around(z, o, NZ), 1 - c, s) for o in range(NZ)}
    x_peer = {o: dev(around(x, o, NX), z, c, s) for o in range(1, NX)}
    y_peer = {o: dev(x, z, c, around(s, o, NY)) for o in range(1, NY)}
    far = (4, 3, 5, 2, 6, 1, 7)
    peers = [*[z_cross[o] for o in far], *[z_peer[o] for o in far], z_cross[0], *x_peer.values(), *y_peer.values()]
    sent = []

    core_of = (1 - c, c)

    def send(src, dst, ssem, rsem, to):
        cp = pltpu.make_async_remote_copy(
            src_ref=src, dst_ref=dst, send_sem=ssem, recv_sem=rsem,
            device_id=to, device_id_type=pl.DeviceIdType.MESH)
        cp.start()
        sent.append(cp)

    def arrived(dst, rsem):
        pltpu.make_async_remote_copy(
            src_ref=dst, dst_ref=dst, send_sem=rsem, recv_sem=rsem,
            device_id=sibling, device_id_type=pl.DeviceIdType.MESH).wait_recv()

    barrier = pltpu.get_barrier_semaphore()
    for peer in peers:
        pl.semaphore_signal(barrier, inc=1, device_id=peer, device_id_type=pl.DeviceIdType.MESH)

    mine = xb.at[c, x, z]
    id_copy = pltpu.make_async_copy(ids_hbm, ids_ref, id_sem)
    tok_copy = pltpu.make_async_copy(tokens_ref, mine.at[:, pl.ds(0, DS)], tok_sem)
    router_copy = pltpu.make_async_copy(router_hbm, router_ref, router_sem)
    w_copies = []
    for e in range(WINDOW):
        for i, (src, dst) in enumerate(((wg_ref, wg), (wu_ref, wu))):
            w_copies.append(pltpu.make_async_copy(src.at[e], dst.at[e], w_sem.at[i, e]))
    for e in range(WINDOW):
        w_copies.append(pltpu.make_async_copy(wd_ref.at[e], wd.at[e], w_sem.at[2, e]))
    for cp in (id_copy, tok_copy, router_copy, *w_copies):
        cp.start()

    id_copy.wait()
    row = lax.broadcasted_iota(jnp.int32, (TOK, 128), 0)
    lane = lax.broadcasted_iota(jnp.int32, (TOK, 128), 1)
    named = jnp.zeros((TOK, 128), jnp.int32)
    for t in range(TOK):
        for k in range(2):
            named = jnp.where((row == t) & (lane == k), ids_ref[k, t], named)
    xb[c, x, z, :, DS:MSG] = named.astype(F32).astype(BF16)
    tok_copy.wait()
    pl.semaphore_wait(barrier, len(peers))

    with jax.named_scope("gather"):
        for o in ALL_Z:
            send(mine, mine, zs.at[o], zr.at[o], z_cross[o])
        for o in ALL_Z:
            block = xb.at[1 - c, x, around(z, -o, NZ)]
            arrived(block, zr.at[o])
            for p in (1, 3, 2):
                send(block, block, xs.at[p - 1, o], xr.at[p - 1], x_peer[p])
            if o:
                send(block, block, cs.at[o - 1], cr.at[o - 1], sibling)
        for p in (1, 3, 2):
            line = xb.at[1 - c, around(x, -p, NX)]
            arrived(line, xr.at[p - 1])
            send(line, line, ks.at[p - 1], kr.at[p - 1], sibling)

    first, second = [None] * CHUNKS, [None] * CHUNKS

    def take_rows(h):
        cores = core_of[h]
        x2d[cores] = xb[cores, :, :, :, 0:DS].reshape(CORE_ROWS, DS)
        ids = xb[cores, :, :, :, DS:MSG].reshape(CORE_ROWS, 128).astype(F32)
        first[h], second[h] = ids[:, 0:1], ids[:, 1:2]

    def gate_up(h):
        for e in range(WINDOW):
            for i, w in enumerate((wg, wu)):
                if h == 0:
                    w_copies[2 * e + i].wait()
                product = jnp.dot(x2d[core_of[h]], w[e], preferred_element_type=F32)
                columns = slice(i * HID, (i + 1) * HID)
                for k, named in enumerate((first[h], second[h])):
                    before = yacc[h, k, :, columns] if e else jnp.zeros((CORE_ROWS, HID), F32)
                    yacc[h, k, :, columns] = jnp.where(named == float(e), product, before)

    def y_send(h):
        for q in range(NY):
            for k in range(2):
                ysend[h, q, k] = yacc[h, k, q * ROWS_Y:(q + 1) * ROWS_Y, :].astype(BF16)
        for p in (2, 1, 3):
            send(ysend.at[h, around(s, p, NY)], ygot.at[h, p - 1], ys.at[h, p - 1], yr.at[h, p - 1], y_peer[p])

    def activate(h):
        for p in (1, 3, 2):
            arrived(ygot.at[h, p - 1], yr.at[h, p - 1])
        for k in range(2):
            total = yacc[h, k, pl.ds(pl.multiple_of(s * ROWS_Y, ROWS_Y), ROWS_Y), :]
            for p in range(1, NY):
                total = total + ygot[h, p - 1, k].astype(F32)
            gate, up = total[:, :HID], total[:, HID:]
            hid[core_of[h], s, k] = (gate / (1.0 + jnp.exp(-gate)) * up).astype(BF16)
        block = hid.at[core_of[h], s]
        for p in (2, 1, 3):
            send(block, block, hs.at[h, p - 1], hr.at[h, p - 1], y_peer[p])

    with jax.named_scope("gate_up"):
        take_rows(0)
        gate_up(0)
        y_send(0)
        for o in Z_ORDER:
            arrived(xb.at[c, x, around(z, -o, NZ)], cr.at[o - 1])
        for p in (1, 3, 2):
            arrived(xb.at[c, around(x, -p, NX)], kr.at[p - 1])
        take_rows(1)
        gate_up(1)
        y_send(1)

    weights = []
    with jax.named_scope("shares"):
        router_copy.wait()
        for i in range(NC):
            lg_own[i] = lax.dot_general(
                router_ref[...], x2d[i], (((1,), (1,)), ((), ())), preferred_element_type=F32)
        for p in range(1, NY):
            send(lg_own, lg_got.at[p - 1], ls.at[p - 1], lr.at[p - 1], y_peer[p])
        activate(0)
        activate(1)
        for p in range(1, NY):
            arrived(lg_got.at[p - 1], lr.at[p - 1])
        expert = lax.broadcasted_iota(jnp.int32, (CORE_ROWS, EXPERTS), 1).astype(F32)
        for h in range(CHUNKS):
            logits = lg_own[core_of[h]]
            for p in range(1, NY):
                logits = logits + lg_got[p - 1, core_of[h]]
            logits = logits.T
            a = jnp.sum(jnp.where(expert == first[h], logits, 0.0), axis=1, keepdims=True)
            b = jnp.sum(jnp.where(expert == second[h], logits, 0.0), axis=1, keepdims=True)
            share_first = 1.0 / (1.0 + jnp.exp(b - a))
            share_second = 1.0 / (1.0 + jnp.exp(a - b))
            weights.append([
                jnp.where(first[h] == float(e), share_first, 0.0)
                + jnp.where(second[h] == float(e), share_second, 0.0) for e in range(WINDOW)])

    def collect(h):
        for p in (1, 3, 2):
            arrived(hid.at[core_of[h], around(s, -p, NY)], hr.at[h, p - 1])
        h0 = hid[core_of[h], :, 0].reshape(CORE_ROWS, HID).astype(F32)
        h1 = hid[core_of[h], :, 1].reshape(CORE_ROWS, HID).astype(F32)
        for e in range(WINDOW):
            rows = jnp.where(first[h] == float(e), h0, jnp.where(second[h] == float(e), h1, 0.0))
            abuf[h, e] = rows.astype(BF16)

    def down(h, n):
        for t in range(COLS // TILE):
            total = None
            for e in range(WINDOW):
                start = n * COLS + t * TILE
                term = weights[h][e] * jnp.dot(
                    abuf[h, e], wd[e, :, start:start + TILE], preferred_element_type=F32)
                total = term if total is None else total + term
            pbuf[n, core_of[h], :, t * TILE:(t + 1) * TILE] = total
        if h == 0:
            send(pbuf.at[n, 1 - c], f1got.at[n], f1s.at[n], f1r.at[n], sibling)

    def along_x(n):
        arrived(f1got.at[n], f1r.at[n])
        total = pbuf[n, c] + f1got[n]
        pbuf[n, c] = total
        for q in range(NX):
            f2send[n, q] = total[q * ROWS_X:(q + 1) * ROWS_X, :].astype(BF16)
        for p in (1, 3, 2):
            send(f2send.at[n, around(x, p, NX)], f2got.at[n, p - 1], f2s.at[n, p - 1], f2r.at[n, p - 1], x_peer[p])

    def along_z(n):
        total = pbuf[n, c, pl.ds(pl.multiple_of(x * ROWS_X, ROWS_X), ROWS_X), :]
        for p in (1, 3, 2):
            arrived(f2got.at[n, p - 1], f2r.at[n, p - 1])
            total = total + f2got[n, p - 1].astype(F32)
        total = total.reshape(NZ, TOK, COLS)
        f3own[n] = total
        f3send[n] = total.astype(BF16)
        for o in Z_ORDER:
            send(f3send.at[n, around(z, o, NZ)], f3got.at[n, o - 1],
                 f3s.at[n, o - 1], f3r.at[n, o - 1], z_peer[o])

    with jax.named_scope("down"):
        for e in range(WINDOW):
            w_copies[2 * WINDOW + e].wait()
        collect(0)
        for n in range(PARTS):
            down(0, n)
    with jax.named_scope("down_own"):
        collect(1)
        for n in range(PARTS):
            down(1, n)
            along_x(n)

    with jax.named_scope("along_z"):
        for n in range(PARTS):
            along_z(n)
        for n in range(PARTS):
            total = f3own[n, z]
            for o in Z_ORDER:
                arrived(f3got.at[n, o - 1], f3r.at[n, o - 1])
                total = total + f3got[n, o - 1].astype(F32)
            out_ref[:, n * COLS:(n + 1) * COLS] = total.astype(BF16)

    for cp in sent:
        cp.wait_send()


def body(tokens, expert_ids, router, w_gate, w_up, w_down):
    vmem, hbm = pl.BlockSpec(memory_space=pltpu.VMEM), pl.BlockSpec(memory_space=pl.ANY)
    dma = pltpu.SemaphoreType.DMA
    scratch = [
        pltpu.VMEM((NC, NX, NZ, TOK, MSG), BF16),
        pltpu.VMEM((NC, CORE_ROWS, DS), BF16),
        pltpu.VMEM((WINDOW, DS, HID), BF16),
        pltpu.VMEM((WINDOW, DS, HID), BF16),
        pltpu.VMEM((WINDOW, HID, DS), BF16),
        pltpu.VMEM((EXPERTS, DS), BF16),
        pltpu.SMEM((2, TOK), jnp.int32),
        pltpu.VMEM((NC, EXPERTS, CORE_ROWS), F32),
        pltpu.VMEM((NY - 1, NC, EXPERTS, CORE_ROWS), F32),
        pltpu.VMEM((CHUNKS, 2, CORE_ROWS, 2 * HID), F32),
        pltpu.VMEM((CHUNKS, NY, 2, ROWS_Y, 2 * HID), BF16),
        pltpu.VMEM((CHUNKS, NY - 1, 2, ROWS_Y, 2 * HID), BF16),
        pltpu.VMEM((NC, NY, 2, ROWS_Y, HID), BF16),
        pltpu.VMEM((CHUNKS, WINDOW, CORE_ROWS, HID), BF16),
        pltpu.VMEM((PARTS, NC, CORE_ROWS, COLS), F32),
        pltpu.VMEM((PARTS, CORE_ROWS, COLS), F32),
        pltpu.VMEM((PARTS, NX, ROWS_X, COLS), BF16),
        pltpu.VMEM((PARTS, NX - 1, ROWS_X, COLS), BF16),
        pltpu.VMEM((PARTS, NZ, TOK, COLS), F32),
        pltpu.VMEM((PARTS, NZ, TOK, COLS), BF16),
        pltpu.VMEM((PARTS, NZ - 1, TOK, COLS), BF16),
        dma, dma, dma, dma((3, WINDOW)),
        dma((NZ,)), dma((NZ,)),
        dma((NX - 1, NZ)), dma((NX - 1,)),
        dma((NZ - 1,)), dma((NZ - 1,)),
        dma((NX - 1,)), dma((NX - 1,)),
        dma((NY - 1,)), dma((NY - 1,)),
        dma((CHUNKS, NY - 1)), dma((CHUNKS, NY - 1)),
        dma((CHUNKS, NY - 1)), dma((CHUNKS, NY - 1)),
        dma((PARTS,)), dma((PARTS,)),
        dma((PARTS, NX - 1)), dma((PARTS, NX - 1)),
        dma((PARTS, NZ - 1)), dma((PARTS, NZ - 1)),
    ]
    flops = 6 * WINDOW * TOKENS * DS * HID
    return pl.pallas_call(
        kernel,
        out_shape=jax.ShapeDtypeStruct((TOK, DS), BF16),
        in_specs=[hbm] * 6,
        out_specs=vmem,
        scratch_shapes=scratch,
        compiler_params=pltpu.CompilerParams(
            collective_id=0, has_side_effects=True, vmem_limit_bytes=60 * 1024 * 1024),
        cost_estimate=pl.CostEstimate(flops=flops, bytes_accessed=6 * WINDOW * DS * HID, transcendentals=0),
    )(tokens, expert_ids.T, router.T, w_gate, w_up, w_down)


def solution(mesh):
    placed = (
        P("dp", "seq"),
        P("dp", None),
        P("seq", None),
        P(None, "seq", "dp"),
        P(None, "seq", "dp"),
        P(None, "dp", "seq"),
    )
    return jax.shard_map(
        body, mesh=mesh, in_specs=placed, out_specs=P("dp", "seq"), check_vma=False
    )
```
